32 devices in a mesh: group: 2 (over y), replica: 4 (over x, core), tensor: 4 (over z).
Axes of the slice: x: 2, y: 2, z: 4, core: 2. Of those that a mesh axis runs over, the one named last changes fastest.
Arguments:
- tokens: bfloat16 [8, 2, 128, 8192], P(('group', 'replica'), None, None, 'tensor'), parts along dimension 0, may hold values from -6 to 6
- merged_query: bfloat16 [8, 8192, 4096], P(('group', 'replica'), None, 'tensor'), parts along dimension 0, may hold values from -0.0625 to 0.0625
- merged_output: bfloat16 [8, 4096, 8192], P(('group', 'replica'), 'tensor'), parts along dimension 0, may hold values from -0.125 to 0.125
- store_wide: bfloat16 [8, 8, 2, 32, 8192], P(('group', 'replica'), None, None, None, 'tensor'), parts along dimension 0, may hold values from -0.59765625 to 0.59765625
- store_narrow: bfloat16 [8, 8, 2, 32, 4096], P(('group', 'replica'), None, None, None, 'tensor'), parts along dimension 0, may hold values from -0.59765625 to 0.59765625
- key_cache: bfloat16 [8, 4, 128, 48, 128], P(('group', 'replica'), 'tensor'), parts along dimension 0, may hold values from -600 to 600, as said below
- value_cache: bfloat16 [8, 4, 128, 48, 128], P(('group', 'replica'), 'tensor'), parts along dimension 0, may hold values from -6 to 6, as said below
- context_length: int32 [8, 128], P(('group', 'replica')), parts along dimension 0, may hold values from 2 to 47
- owner_slot: int32 [32], P('group'), parts along dimension 0, may hold values from 0 to 31, as said below
- old_tenant: int32 [8], P('group'), parts along dimension 0, may hold values from 0 to 15
- new_tenant: int32 [8], P('group'), parts along dimension 0, may hold values from 0 to 15
Outputs:
- attention_out: bfloat16 [8, 2, 128, 8192], P(('group', 'replica'), None, None, 'tensor'), parts along dimension 0
The draws below stay inside these ranges and needn't reach their ends.
There are 2 independent parts, one for each index of `group`. The reference program is written for one: setup_inputs(seed, part) draws one part's arguments, and reference() takes and returns one part's arrays. A program takes and returns all parts, laid end to end along the dimension named above; each array names one. Nothing has to cross between parts.
Inputs may be any that keep to these rules, and one draw needn't show every extreme that they name: `owner_slot`: all values differ; a tenant's adapter lies in replica value // 8, slot value % 8. `key_cache`: entries [j, t] and [j, u] are equal where t == u. `value_cache`: entries [j, t] and [j, u] are equal where t == u.
All inputs are finite; a program needn't handle non-finite values.
Results may differ from the reference program's by a relative error of at most 0.015.
The reference program's roundings to bfloat16 on the way count: a program that leaves them out, or rounds other values in their place, can miss the bound.
Values may be sent and summed in bfloat16 or wider, within the bound.
A program may use at most 256 MiB of HBM per device.

```python
import math
import jax
import jax.numpy as jnp
import numpy as np
from jax import lax

D = 8192
HD = 128
HEADS = 32
KV_HEADS = 4
RANK = 32
STEPS = 2
ROWS = 128
CTX = 48
SLOTS = 8
TEN_REP = 4
TENANTS = 16
KV_COPIES = 1
N_REPLICA = 4
N_TENSOR = 4


def draw_owner_slot(key, part):
    key = jax.random.fold_in(key, 11)
    first_key, second_key = jax.random.split(key)
    slot_total = TENANTS // TEN_REP * SLOTS
    spread = jax.random.permutation(first_key, slot_total - 1)[:TENANTS - 1].astype(jnp.int32)
    picked = jnp.concatenate([spread, jnp.full((1,), slot_total - 1, jnp.int32)])
    tenant_order = jax.random.permutation(second_key, TENANTS)
    return picked[tenant_order].astype(jnp.int32)


def draw_context_length(key, part):
    key = jax.random.fold_in(key, 12)
    first_key, second_key = jax.random.split(key)
    replica_count = TENANTS // TEN_REP
    highest = CTX - STEPS + 1
    lengths = jax.random.randint(first_key, (replica_count * ROWS,), 2, highest + 1).astype(jnp.int32)
    spot_index = jax.random.randint(second_key, (), 0, replica_count * ROWS)
    lengths = lengths.at[spot_index].set(highest)
    return lengths.reshape(replica_count, ROWS).astype(jnp.int32)


def draw_key_cache(key, part):
    key = jax.random.fold_in(key, 13)
    replica_count = TENANTS // TEN_REP
    draw_shape = (replica_count, KV_HEADS, ROWS, CTX, HD)
    base_key = jax.random.fold_in(key, 0)
    base_field = jax.random.normal(base_key, draw_shape, jnp.float32)
    return jnp.repeat(base_field, KV_COPIES, axis=1).astype(jnp.bfloat16)


def draw_value_cache(key, part):
    key = jax.random.fold_in(key, 14)
    replica_count = TENANTS // TEN_REP
    draw_shape = (replica_count, KV_HEADS, ROWS, CTX, HD)
    base_field = jnp.clip(jax.random.normal(key, draw_shape, jnp.float32), -6.0, 6.0)
    return jnp.repeat(base_field, KV_COPIES, axis=1).astype(jnp.bfloat16)


def with_ends(drawn, stream_key, smallest, top_value):
    longest = drawn.shape.index(max(drawn.shape))
    spots = []
    for shift in (0, 1):
        where = [jax.random.randint(jax.random.fold_in(stream_key, axis), (), 0, length) for axis, length in enumerate(drawn.shape)]
        where[longest] = (where[longest] + shift) % drawn.shape[longest]
        spots.append(tuple(where))
    return drawn.at[spots[0]].set(smallest).at[spots[1]].set(top_value)


def with_spikes(drawn, key, source, target, shards_of, factor):
    owner, partner = [(jnp.arange(drawn.shape[position]) // (drawn.shape[position] // shards_of)).reshape([-1 if axis == position else 1 for axis in range(drawn.ndim)]) for position in (source, target)]
    chosen = jax.random.permutation(key, shards_of)[partner]
    strong = (owner == chosen) | (owner == (partner + shards_of // 2) % shards_of)
    return jnp.where(strong, factor * drawn, drawn)


def shard_levels(own_key, shape, pieces, least, largest):
    level, own = 1.0, jax.random.fold_in(own_key, 6)
    for position, parts in pieces:
        heights = jnp.exp(jax.random.uniform(jax.random.fold_in(own, position), (parts,), jnp.float32, least / len(pieces), largest / len(pieces)))
        level = level * jnp.repeat(heights, shape[position] // parts).reshape([-1 if axis == position else 1 for axis in range(len(shape))])
    return level


def rank_bounds(number_of, slope):
    weights = [(1 << 20) // math.isqrt(rank ** slope) + 1 for rank in range(1, number_of + 1)]
    scale = 1 + sum(weights) // (1 << 30)
    return np.cumsum(np.array([max(1, weight // scale) for weight in weights]))


def ranked_ids(stream_key, shape, number_of, lean):
    grid = rank_bounds(number_of, lean)
    ticket = jax.random.randint(jax.random.fold_in(stream_key, 1), shape, 0, int(grid[number_of - 1]))
    standing = jnp.searchsorted(jnp.asarray(grid, jnp.int32), ticket, side="right")
    return jax.random.permutation(jax.random.fold_in(stream_key, 2), number_of)[standing].astype(jnp.int32)


def centred(key, dims, scale, limit, cuts=(), held_as=jnp.bfloat16):
    array = scale * jax.random.normal(key, dims, jnp.float32)
    if cuts:
        array = array * shard_levels(key, dims, cuts, -0.22, 0.18)
    return jnp.clip(array, -limit, limit).astype(held_as)


def noise_with(stream_key, dims, scale, most, shards, heavy, kind=jnp.bfloat16):
    values = scale * jax.random.normal(stream_key, dims, jnp.float32)
    if shards:
        values = values * shard_levels(stream_key, dims, shards, -0.22, 0.18)
    return jnp.clip(with_spikes(values, jax.random.fold_in(stream_key, 3), *heavy), -most, most).astype(kind)


def setup_inputs(seed: int = 0, part: int = 0) -> dict:
    keys = jax.random.split(jax.random.key(seed), 12)
    own_keys = jax.random.split(jax.random.fold_in(keys[11], part), 12)
    tokens = centred(own_keys[0], (N_REPLICA, STEPS, ROWS, D), 1.0, 6.0, ((0, 4), (3, 4)))
    merged_query = centred(own_keys[1], (N_REPLICA, D, HEADS * HD), D ** -0.5, 0.0625, ((0, 4), (2, 4)))
    merged_output = noise_with(own_keys[2], (N_REPLICA, HEADS * HD, D), (HEADS * HD) ** -0.5, 0.125, ((0, 4), (1, 4)), (1, 2, 4, 2.0))
    store_wide = centred(own_keys[3], (N_REPLICA, SLOTS, 2, RANK, D), 0.1, 0.59765625, ((0, 4), (4, 4)))
    store_narrow = centred(own_keys[4], (N_REPLICA, SLOTS, 2, RANK, HEADS * HD), 0.1, 0.59765625, ((0, 4), (4, 4)))
    key_cache = draw_key_cache(jax.random.fold_in(jax.random.fold_in(keys[11], part), 71), part)
    value_cache = draw_value_cache(jax.random.fold_in(jax.random.fold_in(keys[11], part), 71), part)
    context_length = draw_context_length(jax.random.fold_in(jax.random.fold_in(keys[11], part), 71), part)
    owner_slot = draw_owner_slot(jax.random.fold_in(jax.random.fold_in(keys[11], part), 71), part)
    old_tenant = with_ends(jax.random.randint(own_keys[9], (N_REPLICA,), 0, TENANTS), jax.random.fold_in(own_keys[9], 1), 0, TENANTS - 1).astype(jnp.int32)
    new_tenant = with_ends(ranked_ids(own_keys[10], (N_REPLICA,), TENANTS, 2), jax.random.fold_in(own_keys[10], 3), 0, TENANTS - 1).astype(jnp.int32)
    return dict(tokens=tokens, merged_query=merged_query, merged_output=merged_output, store_wide=store_wide, store_narrow=store_narrow, key_cache=key_cache, value_cache=value_cache, context_length=context_length, owner_slot=owner_slot, old_tenant=old_tenant, new_tenant=new_tenant)


adapter_scale = 0.25


def outer_product(left_factor, right_factor):
    return lax.dot_general(left_factor, right_factor, (((0,), (0,)), ((), ())), preferred_element_type=jnp.float32)


def attend(queries, key_rows, value_rows, visible):
    shaped = queries.reshape(ROWS, N_TENSOR, HEADS // N_TENSOR, HD).astype(jnp.float32)
    scores = jnp.einsum('rgqd,grcd->gqrc', shaped, key_rows.astype(jnp.float32)) * (HD ** -0.5)
    scores = jnp.where(visible[None, None], scores, -jnp.inf)
    highest = jnp.max(scores, axis=3, keepdims=True)
    weights = jnp.exp(scores - highest)
    probability = (weights / jnp.sum(weights, axis=3, keepdims=True)).astype(jnp.bfloat16)
    blended = jnp.einsum('gqrc,grcd->rgqd', probability.astype(jnp.float32), value_rows.astype(jnp.float32))
    return blended.astype(jnp.bfloat16).reshape(ROWS, HEADS * HD)


def reference(tokens, merged_query, merged_output, store_wide, store_narrow, key_cache, value_cache, context_length, owner_slot, old_tenant, new_tenant):
    wide_flat = store_wide.reshape(N_REPLICA * SLOTS, 2, RANK, D)
    narrow_flat = store_narrow.reshape(N_REPLICA * SLOTS, 2, RANK, HEADS * HD)
    group_width = HEADS * HD // N_TENSOR
    positions = jnp.arange(CTX, dtype=jnp.int32)
    replica_outputs = []
    for replica in range(N_REPLICA):
        old_index = owner_slot[old_tenant[replica]]
        new_index = owner_slot[new_tenant[replica]]
        old_wide = wide_flat[old_index]
        new_wide = wide_flat[new_index]
        old_narrow = narrow_flat[old_index]
        new_narrow = narrow_flat[new_index]
        weight_query = (merged_query[replica].astype(jnp.float32) + adapter_scale * outer_product(new_wide[0], new_narrow[0]) - adapter_scale * outer_product(old_wide[0], old_narrow[0])).astype(jnp.bfloat16)
        weight_output = (merged_output[replica].astype(jnp.float32) + adapter_scale * outer_product(new_narrow[1], new_wide[1]) - adapter_scale * outer_product(old_narrow[1], old_wide[1])).astype(jnp.bfloat16)
        step_outputs = []
        for step_index in range(STEPS):
            queries = jnp.dot(tokens[replica, step_index], weight_query, preferred_element_type=jnp.float32).astype(jnp.bfloat16)
            visible = positions[None, :] < (context_length[replica] + step_index)[:, None]
            contexts = attend(queries, key_cache[replica], value_cache[replica], visible)
            summed = jnp.zeros((ROWS, D), jnp.float32)
            for group_index in range(N_TENSOR):
                lower = group_index * group_width
                partial_sum = jnp.dot(contexts[:, lower:lower + group_width], weight_output[lower:lower + group_width], preferred_element_type=jnp.float32)
                summed = summed + lax.optimization_barrier(partial_sum.astype(jnp.bfloat16)).astype(jnp.float32)
            step_outputs.append(summed.astype(jnp.bfloat16))
        replica_outputs.append(jnp.stack(step_outputs, 0))
    return jnp.stack(replica_outputs, 0)
```

```python
import functools

import jax
import jax.numpy as jnp
from jax import lax
from jax.experimental import pallas as pl
from jax.experimental.pallas import tpu as pltpu
from jax.sharding import PartitionSpec as P

adapter_scale = 0.25
CHUNKS = 4
GROUP = 8
MESH = pl.DeviceIdType.MESH
F32 = jnp.float32
BF16 = jnp.bfloat16


def nt_dot(left, right):
    return lax.dot_general(left, right, (((1,), (1,)), ((), ())), preferred_element_type=F32)


def kernel(
    n, nr, steps, rows, width, narrow, head_size, ctx, slots, rank,
    owner_ref, old_ref, new_ref, upper_ref,
    tokens_hbm, wq_hbm, wo_hbm, wide_hbm, narrow_hbm, key_hbm, value_hbm,
    out_ref,
    wq, wo, wide, nar, key, value, tok, part, qacc, ctxs, total,
    send_ad, recv_ad, ad, zbuf, ybuf,
    wq_sem, wo_sem, store_sem, kv_sem, tok_sem,
    ag_send, ag_recv, rs_send, rs_recv, ad_send, ad_recv, z_send, z_recv, y_send, y_recv,
):
    z = lax.axis_index("tensor")
    me_r = lax.axis_index("replica")
    chunk_rows = rows // CHUNKS
    chunk = steps * chunk_rows
    heads = narrow // head_size
    keys = GROUP * ctx

    def token_copy(c, s):
        return pltpu.make_async_copy(
            tokens_hbm.at[s, pl.ds(c * chunk_rows, chunk_rows)],
            tok.at[c, z, pl.ds(s * chunk_rows, chunk_rows)],
            tok_sem.at[c, s],
        )

    for c in range(CHUNKS):
        for s in range(steps):
            token_copy(c, s).start()
    wide_copy = pltpu.make_async_copy(wide_hbm, wide, store_sem.at[0])
    nar_copy = pltpu.make_async_copy(narrow_hbm, nar, store_sem.at[1])
    wide_copy.start()
    nar_copy.start()

    def wq_copy(b):
        return pltpu.make_async_copy(wq_hbm.at[b], wq.at[b], wq_sem.at[b])

    def wo_copy(b):
        return pltpu.make_async_copy(
            wo_hbm.at[:, pl.ds(b * width, width)], wo.at[b], wo_sem.at[b]
        )

    for b in range(n):
        wq_copy(b).start()
    key_copy = pltpu.make_async_copy(key_hbm, key, kv_sem.at[0])
    value_copy = pltpu.make_async_copy(value_hbm, value, kv_sem.at[1])
    key_copy.start()
    value_copy.start()
    for b in range(n):
        wo_copy(b).start()

    barrier = pltpu.get_barrier_semaphore()

    @pl.loop(1, n)
    def _(k):
        pl.semaphore_signal(barrier, inc=1, device_id={"tensor": lax.rem(z + k, n)}, device_id_type=MESH)

    @pl.loop(1, nr)
    def _(k):
        pl.semaphore_signal(barrier, inc=1, device_id={"replica": lax.rem(me_r + k, nr)}, device_id_type=MESH)

    pl.semaphore_wait(barrier, n - 1 + nr - 1)

    def ag_copy(c, b, way):
        return pltpu.make_async_remote_copy(
            src_ref=tok.at[c, b], dst_ref=tok.at[c, b],
            send_sem=ag_send.at[c, b, way], recv_sem=ag_recv.at[c, b],
            device_id={"tensor": z + 1 if way == 0 else z - 1}, device_id_type=MESH,
        )

    for c in range(CHUNKS):
        for s in range(steps):
            token_copy(c, s).wait()

    def send_own(c):
        @pl.when(z < n - 1)
        def _():
            ag_copy(c, z, 0).start()

        @pl.when(z > 0)
        def _():
            ag_copy(c, z, 1).start()

    send_own(0)

    wide_copy.wait()
    nar_copy.wait()

    def ad_copy(side, j):
        return pltpu.make_async_remote_copy(
            src_ref=send_ad.at[side, j], dst_ref=recv_ad.at[side, me_r],
            send_sem=ad_send.at[side, j], recv_sem=ad_recv.at[side, me_r],
            device_id={"replica": j}, device_id_type=MESH,
        )

    def ad_arrival(side, j):
        return pltpu.make_async_remote_copy(
            src_ref=send_ad.at[side, j], dst_ref=recv_ad.at[side, j],
            send_sem=ad_send.at[side, j], recv_sem=ad_recv.at[side, j],
            device_id={"replica": j}, device_id_type=MESH,
        )

    for side in range(2):
        @pl.loop(1, nr + 1)
        def _(k, side=side):
            j = lax.rem(me_r + k, nr)
            for w, tenant_ref in ((0, old_ref), (1, new_ref)):
                place = owner_ref[tenant_ref[j]]
                mine = (place // slots == me_r).astype(F32)
                slot = place % slots
                spot = pl.ds(w * rank, rank)
                send_ad[side, j, spot, 0:width] = (wide[slot, side].astype(F32) * mine).astype(BF16)
                send_ad[side, j, spot, width:] = (nar[slot, side].astype(F32) * mine).astype(BF16)

            @pl.when(k < nr)
            def _():
                ad_copy(side, j).start()

    def take_adapter(side):
        ad[side, 0:2 * rank] = send_ad[side, me_r]
        ad[side, 2 * rank:] = jnp.zeros_like(ad[side, 2 * rank:])

        @pl.loop(1, nr)
        def _(k):
            j = lax.rem(me_r + k, nr)
            ad_arrival(side, j).wait_recv()
            ad[side, 0:2 * rank] += recv_ad[side, j]

    lane = lax.broadcasted_iota(jnp.int32, (chunk, 128), 1)
    factor = jnp.where(lane < rank, -adapter_scale, adapter_scale).astype(F32)

    def low_rank(pieces, matrix):
        mixed = pieces * factor
        high = mixed.astype(BF16)
        low = (mixed - high.astype(F32)).astype(BF16)
        return (
            jnp.dot(high, matrix, preferred_element_type=F32)
            + jnp.dot(low, matrix, preferred_element_type=F32)
        )

    def z_copy(peer):
        return pltpu.make_async_remote_copy(
            src_ref=zbuf.at[z], dst_ref=zbuf.at[z], send_sem=z_send.at[peer],
            recv_sem=z_recv.at[z], device_id={"tensor": peer}, device_id_type=MESH,
        )

    def z_arrival(peer):
        return pltpu.make_async_remote_copy(
            src_ref=zbuf.at[peer], dst_ref=zbuf.at[peer], send_sem=z_send.at[peer],
            recv_sem=z_recv.at[peer], device_id={"tensor": peer}, device_id_type=MESH,
        )

    def y_copy(c, peer):
        return pltpu.make_async_remote_copy(
            src_ref=ybuf.at[c, z], dst_ref=ybuf.at[c, z], send_sem=y_send.at[c, peer],
            recv_sem=y_recv.at[c, z], device_id={"tensor": peer}, device_id_type=MESH,
        )

    def y_arrival(c, peer):
        return pltpu.make_async_remote_copy(
            src_ref=ybuf.at[c, peer], dst_ref=ybuf.at[c, peer], send_sem=y_send.at[c, peer],
            recv_sem=y_recv.at[c, peer], device_id={"tensor": peer}, device_id_type=MESH,
        )

    q_tile = min(narrow, 512)
    o_tile = min(width, 512)

    def project(c, b, first):
        @pl.when(c == 0)
        def _():
            wq_copy(b).wait()

        @pl.loop(0, narrow // q_tile)
        def _(t):
            cols = pl.ds(pl.multiple_of(t * q_tile, q_tile), q_tile)
            product = jnp.dot(tok[c, b], wq[b, :, cols], preferred_element_type=F32)
            if first:
                qacc[:, cols] = product
            else:
                qacc[:, cols] += product

    def rs_copy(c, b, source, way):
        slot = b if way == 0 else jnp.where(b == z - 1, n, b)
        return pltpu.make_async_remote_copy(
            src_ref=source.at[c, b], dst_ref=part.at[c, slot],
            send_sem=rs_send.at[c, b], recv_sem=rs_recv.at[c, slot],
            device_id={"tensor": z + 1 if way == 0 else z - 1}, device_id_type=MESH,
        )

    def rs_arrival(c, slot):
        return pltpu.make_async_remote_copy(
            src_ref=part.at[c, slot], dst_ref=part.at[c, slot],
            send_sem=rs_send.at[c, 0], recv_sem=rs_recv.at[c, slot],
            device_id={"tensor": lax.rem(z + 1, n)}, device_id_type=MESH,
        )

    def rs_pass(c, b, way):
        rs_arrival(c, b).wait_recv()
        part[c, b] = (part[c, b].astype(F32) + tok[c, b].astype(F32)).astype(BF16)
        rs_copy(c, b, part, way).start()

    def rs_step(c, i):
        far = n - 1 - i

        @pl.when(jnp.logical_and(z > 0, far > z))
        def _():
            rs_pass(c, far, 0)

        @pl.when(jnp.logical_and(z < n - 1, i < z))
        def _():
            rs_pass(c, i, 1)

    def finish(c):
        @pl.loop(1, n)
        def _(k):
            y_arrival(c, lax.rem(z + k, n)).wait_recv()

        mixed = ybuf[c, 0].astype(F32)
        for b in range(1, n):
            mixed = mixed + ybuf[c, b].astype(F32)
        total[...] = tok[c, z].astype(F32) + low_rank(mixed, ad[1, :, 0:width])

        @pl.when(z > 0)
        def _():
            rs_arrival(c, z).wait_recv()
            total[...] += part[c, z].astype(F32)

        @pl.when(z < n - 1)
        def _():
            rs_arrival(c, n).wait_recv()
            total[...] += part[c, n].astype(F32)

        for s in range(steps):
            out_ref[s, pl.ds(pl.multiple_of(c * chunk_rows, chunk_rows), chunk_rows)] = total[
                s * chunk_rows:(s + 1) * chunk_rows
            ].astype(BF16)

    def attention(c):
        queries_in_group = heads * steps * GROUP
        row = lax.broadcasted_iota(jnp.int32, (queries_in_group, keys), 0)
        column = lax.broadcasted_iota(jnp.int32, (queries_in_group, keys), 1)
        lowest = (row % GROUP) * ctx

        @pl.loop(0, chunk_rows // GROUP)
        def _(g):
            place = c * (chunk_rows // GROUP) + g

            def spot(s):
                return pl.ds(pl.multiple_of(s * chunk_rows + g * GROUP, GROUP), GROUP)

            pieces = [
                qacc[spot(s), h * head_size:(h + 1) * head_size]
                for h in range(heads) for s in range(steps)
            ]
            queries = jnp.concatenate(pieces, axis=0).astype(BF16)
            scores = nt_dot(queries, key[place]) * head_size ** (-0.5)
            visible = jnp.logical_and(column >= lowest, column < upper_ref[place])
            scores = jnp.where(visible, scores, -1e30)
            highest = jnp.max(scores, axis=1, keepdims=True)
            weights = jnp.exp(scores - highest)
            weights = jnp.where(visible, weights, 0.0)
            probability = (weights / jnp.sum(weights, axis=1, keepdims=True)).astype(BF16)
            blended = jnp.dot(probability, value[place], preferred_element_type=F32)
            index = 0
            for h in range(heads):
                for s in range(steps):
                    ctxs[spot(s), h * head_size:(h + 1) * head_size] = blended[
                        index * GROUP:(index + 1) * GROUP
                    ]
                    index += 1

    @pl.loop(0, CHUNKS)
    def _(c):
        @pl.when(c + 1 < CHUNKS)
        def _():
            send_own(c + 1)

        project(c, z, True)

        @pl.loop(1, n)
        def _(d):
            left, right = z - d, z + d

            @pl.when(left >= 0)
            def _():
                ag_copy(c, left, 1).wait_recv()

                @pl.when(z < n - 1)
                def _():
                    ag_copy(c, left, 0).start()

            @pl.when(right < n)
            def _():
                ag_copy(c, right, 0).wait_recv()

                @pl.when(z > 0)
                def _():
                    ag_copy(c, right, 1).start()

            @pl.when(c > 0)
            def _():
                rs_step(c - 1, d - 1)

            @pl.when(left >= 0)
            def _():
                project(c, left, False)

            @pl.when(right < n)
            def _():
                project(c, right, False)

        @pl.when(c == 0)
        def _():
            take_adapter(0)
            for k in range(CHUNKS):
                zbuf[z, k * chunk:(k + 1) * chunk] = nt_dot(tok[k, z], ad[0, :, 0:width]).astype(BF16)

            @pl.loop(1, n)
            def _(k):
                z_copy(lax.rem(z + k, n)).start()

            take_adapter(1)
            key_copy.wait()
            value_copy.wait()

            @pl.loop(1, n)
            def _(k):
                z_arrival(lax.rem(z + k, n)).wait_recv()

        mine = pl.ds(pl.multiple_of(c * chunk, chunk), chunk)
        mixed = zbuf[0, mine].astype(F32)
        for b in range(1, n):
            mixed = mixed + zbuf[b, mine].astype(F32)
        qacc[...] += low_rank(mixed, ad[0, :, width:])
        attention(c)
        contexts = ctxs[...].astype(BF16)
        ybuf[c, z] = nt_dot(contexts, ad[1, :, width:]).astype(BF16)

        @pl.loop(1, n)
        def _(k):
            y_copy(c, lax.rem(z + k, n)).start()

        @pl.loop(0, n)
        def _(b):
            @pl.when(jnp.logical_and(z < n - 1, b <= z))
            def _():
                ag_copy(c, b, 0).wait_send()

            @pl.when(jnp.logical_and(z > 0, b >= z))
            def _():
                ag_copy(c, b, 1).wait_send()

        @pl.loop(0, n)
        def _(i):
            b = jnp.where(i % 2 == 0, n - 1 - i // 2, i // 2)

            @pl.when(c == 0)
            def _():
                wo_copy(b).wait()

            @pl.loop(0, width // o_tile)
            def _(t):
                cols = pl.ds(pl.multiple_of(t * o_tile, o_tile), o_tile)
                tok[c, b, :, cols] = jnp.dot(
                    ctxs[...].astype(BF16), wo[b, :, cols], preferred_element_type=F32
                ).astype(BF16)

            @pl.when(jnp.logical_and(z == 0, b > 0))
            def _():
                rs_copy(c, b, tok, 0).start()

            @pl.when(jnp.logical_and(z == n - 1, b < n - 1))
            def _():
                rs_copy(c, b, tok, 1).start()

        @pl.when(c > 0)
        def _():
            finish(c - 1)

    @pl.loop(0, n - 1)
    def _(i):
        rs_step(CHUNKS - 1, i)

    finish(CHUNKS - 1)

    @pl.loop(1, n)
    def _(k):
        peer = lax.rem(z + k, n)
        z_copy(peer).wait_send()

        @pl.loop(0, CHUNKS)
        def _(c):
            y_copy(c, peer).wait_send()
            rs_copy(c, peer, part, 0).wait_send()

    @pl.loop(1, nr)
    def _(k):
        j = lax.rem(me_r + k, nr)
        for side in range(2):
            ad_copy(side, j).wait_send()


def on_device(
    tokens, merged_query, merged_output, store_wide, store_narrow,
    key_cache, value_cache, context_length, owner_slot, old_tenant, new_tenant,
):
    n, nr = lax.axis_size("tensor"), lax.axis_size("replica")
    steps, rows, width = tokens.shape[1:]
    narrow = merged_query.shape[2]
    slots, _, rank, _ = store_wide.shape[1:]
    ctx, head_size = key_cache.shape[3:]
    heads = narrow // head_size
    groups = rows // GROUP
    chunk_rows = rows // CHUNKS
    chunk = steps * chunk_rows
    upper = (
        context_length.reshape(groups, 1, 1, GROUP)
        + jnp.arange(steps, dtype=jnp.int32)[None, None, :, None]
        + ctx * jnp.arange(GROUP, dtype=jnp.int32)
    )
    upper = jnp.broadcast_to(upper, (groups, heads, steps, GROUP)).reshape(groups, -1, 1)
    hbm = pl.BlockSpec(memory_space=pl.ANY)
    smem = pl.BlockSpec(memory_space=pltpu.SMEM)
    vmem = pl.BlockSpec(memory_space=pltpu.VMEM)
    dma = pltpu.SemaphoreType.DMA
    result = pl.pallas_call(
        functools.partial(
            kernel, n, nr, steps, rows, width, narrow, head_size, ctx, slots, rank
        ),
        out_shape=jax.ShapeDtypeStruct((steps, rows, width), BF16),
        in_specs=[smem] * 3 + [vmem] + [hbm] * 7,
        out_specs=vmem,
        scratch_shapes=[
            pltpu.VMEM((n, width, narrow), BF16),
            pltpu.VMEM((n, narrow, width), BF16),
            pltpu.VMEM((slots, 2, rank, width), BF16),
            pltpu.VMEM((slots, 2, rank, narrow), BF16),
            pltpu.VMEM((groups, GROUP * ctx, head_size), BF16),
            pltpu.VMEM((groups, GROUP * ctx, head_size), BF16),
            pltpu.VMEM((CHUNKS, n, chunk, width), BF16),
            pltpu.VMEM((CHUNKS, n + 1, chunk, width), BF16),
            pltpu.VMEM((chunk, narrow), F32),
            pltpu.VMEM((chunk, narrow), F32),
            pltpu.VMEM((chunk, width), F32),
            pltpu.VMEM((2, nr, 2 * rank, width + narrow), BF16),
            pltpu.VMEM((2, nr, 2 * rank, width + narrow), BF16),
            pltpu.VMEM((2, 128, width + narrow), BF16),
            pltpu.VMEM((n, CHUNKS * chunk, 128), BF16),
            pltpu.VMEM((CHUNKS, n, chunk, 128), BF16),
            dma((n,)), dma((n,)), dma((2,)), dma((2,)), dma((CHUNKS, steps)),
            dma((CHUNKS, n, 2)), dma((CHUNKS, n)),
            dma((CHUNKS, n)), dma((CHUNKS, n + 1)),
            dma((2, nr)), dma((2, nr)),
            dma((n,)), dma((n,)), dma((CHUNKS, n)), dma((CHUNKS, n)),
        ],
        compiler_params=pltpu.CompilerParams(
            collective_id=0, has_side_effects=True, vmem_limit_bytes=63 * 2 ** 20
        ),
    )(
        owner_slot, old_tenant, new_tenant, upper,
        tokens[0], merged_query[0].reshape(n, width, narrow), merged_output[0],
        store_wide[0], store_narrow[0],
        key_cache[0, 0].reshape(groups, GROUP * ctx, head_size),
        value_cache[0, 0].reshape(groups, GROUP * ctx, head_size),
    )
    return result[None]


def solution(mesh):
    return jax.shard_map(
        on_device,
        mesh=mesh,
        in_specs=(
            P(("group", "replica"), None, None, "tensor"),
            P(("group", "replica"), None, "tensor"),
            P(("group", "replica"), "tensor", None),
            P(("group", "replica"), None, None, None, "tensor"),
            P(("group", "replica"), None, None, None, "tensor"),
            P(("group", "replica"), "tensor", None, None, None),
            P(("group", "replica"), "tensor", None, None, None),
            P(("group", "replica"), None),
            P("group"),
            P("group"),
            P("group"),
        ),
        out_specs=P(("group", "replica"), None, None, "tensor"),
        check_vma=False,
    )
```
